512 devices in a mesh: gr: 16 (over y, z_hi, core), gc: 32 (over z_lo, x).
Axes of the slice: x: 4, y: 4, z: 16 (z_hi: 2, z_lo: 8; z = z_hi * 8 + z_lo), core: 2. Of those that a mesh axis runs over, the one named last changes fastest.
Arguments:
- grad: bfloat16 [640, 16384], P('gc', 'gr'), may hold values from -6 to 6
- basis: bfloat16 [16384, 16384], P('gr', 'gc'), may hold values from -0.046875 to 0.046875
- first_moment: float32 [640, 16384], P('gr', 'gc'), may hold values from -3 to 3
- second_moment: float32 [640, 16384], P('gr', 'gc'), may hold values from 0.001 to 0.1
Outputs:
- update: bfloat16 [640, 16384], P('gc', 'gr')
- new_first: float32 [640, 16384], P('gr', 'gc')
- new_second: float32 [640, 16384], P('gr', 'gc')
The draws below stay inside these ranges and needn't reach their ends.
All inputs are finite; a program needn't handle non-finite values.
Results may differ from the reference program's by a relative error of at most 0.0049.
Values may be sent and summed in bfloat16 or wider, within the bound.
No kernel may reach another device: no remote copies, remote signals or barrier semaphores. Data moves between devices by JAX's collectives and lax.ppermute only.
A program may use at most 64 MiB of HBM per device.

```python
import math
import jax
import jax.numpy as jnp
from jax import lax

FF = 16384
ROWS = 640
STEP = 10


def block_scale(stream_key, shape, pieces, smallest, high):
    factor_of = 1.0
    for dim, blocks in pieces:
        heights = jax.random.uniform(jax.random.fold_in(jax.random.fold_in(stream_key, 6), dim), (blocks,), jnp.float32, smallest / len(pieces), high / len(pieces))
        factor_of = factor_of * jnp.repeat(jnp.exp(heights), shape[dim] // blocks).reshape((-1,) + (1,) * (len(shape) - 1 - dim))
    return factor_of


def scatter_about(rng, shape, spread, limit, pieces=(), kind=jnp.bfloat16):
    values = jax.random.normal(rng, shape, jnp.float32) * spread
    if len(pieces) > 0:
        values = block_scale(rng, shape, pieces, -0.22, 0.18) * values
    return jnp.clip(values, min=-limit, max=limit).astype(kind)


def setup_inputs(seed: int = 0) -> dict:
    seeds = jax.random.split(jax.random.key(seed), 5)
    grad = scatter_about(seeds[0], (ROWS, FF), 1.0, 6.0, ((0, 32), (1, 16)))
    basis = scatter_about(seeds[1], (FF, FF), FF ** -0.5, 0.046875, ((0, 16), (1, 32)))
    first_moment = scatter_about(seeds[2], (ROWS, FF), 0.5, 3.0, ((0, 16), (1, 32)), jnp.float32)
    second_moment = jnp.clip(jnp.exp(math.log(0.1) - 4.6051702 * jax.random.uniform(seeds[3], (ROWS, FF), jnp.float32) ** block_scale(seeds[3], (ROWS, FF), ((0, 16), (1, 32)), -0.2, 0.2)), 0.001, 0.1)
    return {"grad": grad, "basis": basis, "first_moment": first_moment, "second_moment": second_moment}


BETA_ONE = 0.9
BETA_TWO = 0.999
EPSILON = 1e-08

def reference(grad, basis, first_moment, second_moment):
    rotated = jnp.dot(grad, basis, preferred_element_type=jnp.float32)
    new_first = BETA_ONE * first_moment + (1.0 - BETA_ONE) * rotated
    new_second = BETA_TWO * second_moment + (1.0 - BETA_TWO) * rotated * rotated
    corr_one = 1.0 - BETA_ONE ** STEP
    corr_two = 1.0 - BETA_TWO ** STEP
    direction = (new_first / corr_one / (jnp.sqrt(new_second / corr_two) + EPSILON)).astype(jnp.bfloat16)
    total = lax.dot_general(direction, basis, (((1,), (1,)), ((), ())), preferred_element_type=jnp.float32)
    return (total.astype(jnp.bfloat16), new_first, new_second)
```

```python
import jax
import jax.numpy as jnp
from jax import lax
from jax.sharding import Mesh
from jax.sharding import PartitionSpec as P

STEP = 10


BETA_ONE = 0.9
BETA_TWO = 0.999
EPSILON = 1e-08

F32, BF16 = jnp.float32, jnp.bfloat16
LANES = 128
SIZES = {"y": 4, "zh": 2, "core": 2, "zf": 4, "zn": 2, "x": 4}
GR = ("y", "zh", "core")
GC = ("zf", "zn", "x")


def adam_step(rotated, first_moment, second_moment):
    new_first = BETA_ONE * first_moment + (1.0 - BETA_ONE) * rotated
    new_second = BETA_TWO * second_moment + (1.0 - BETA_TWO) * rotated * rotated
    corr_one = 1.0 - BETA_ONE**STEP
    corr_two = 1.0 - BETA_TWO**STEP
    direction = (new_first / corr_one / (jnp.sqrt(new_second / corr_two) + EPSILON)).astype(BF16)
    return (direction, new_first, new_second)


def spread(block, axes, n):
    return lax.all_to_all(jnp.broadcast_to(block[None], (n,) + block.shape), axes, 0, 0, tiled=True)


def swap(value, axis):
    return lax.ppermute(value, axis, [(0, 1), (1, 0)])


def shards(grad, basis, first_moment, second_moment):
    zh = lax.axis_index("zh")
    rows, cols = grad.shape
    first_other = swap(first_moment, "zh")
    second_other = swap(second_moment, "zh")

    block = grad.reshape(rows, cols // LANES, LANES)
    block = spread(block, "zf", 4)
    block = spread(block, ("zn", "x"), 8)
    block = block.reshape(2, 2, 2, 4, rows, cols // LANES, LANES)
    picked = block.transpose(3, 1, 0, 2, 4, 5, 6).reshape(32 * rows, cols)

    partial = jnp.dot(picked, basis, preferred_element_type=F32).astype(BF16)
    parts = lax.all_to_all(partial.reshape(8, 80, -1), ("y", "core"), 0, 0, tiled=True)
    parts, first_other, second_other = lax.optimization_barrier((parts, first_other, second_other))
    part = jnp.sum(parts.astype(F32), axis=0)
    rotated = part + swap(part.astype(BF16), "zh").astype(F32)
    low, high = rotated[:40], rotated[40:]
    first = zh == 0
    mine, other = jnp.where(first, low, high), jnp.where(first, high, low)
    share, new_first, new_second = adam_step(mine, first_moment, second_moment)
    share_other, _, _ = adam_step(other, first_other, second_other)
    pair = jnp.concatenate(
        [jnp.where(first, share, share_other), jnp.where(first, share_other, share)], axis=0
    )
    direction = lax.all_gather(pair, ("y", "core"), axis=0, tiled=True)

    total = lax.dot_general(
        direction, basis, (((1,), (1,)), ((), ())), preferred_element_type=F32
    ).astype(BF16)
    total = total.reshape(4, 2, 2, 2, rows, cols // LANES, LANES)
    total = total.transpose(2, 1, 3, 0, 4, 5, 6).reshape(8, 4, rows, cols // LANES, LANES)
    total = lax.all_to_all(total, ("zn", "x"), 0, 0, tiled=True)
    total = jnp.sum(total.astype(F32), axis=0).astype(BF16)
    total = lax.all_to_all(total, "zf", 0, 0, tiled=True)
    update = jnp.sum(total.astype(F32), axis=0).astype(BF16).reshape(rows, cols)
    return (update, new_first, new_second)


def solution(mesh):
    fine = Mesh(mesh.devices.reshape(tuple(SIZES.values())), tuple(SIZES))
    in_specs = (P(GC, GR), P(GR, GC), P(GR, GC), P(GR, GC))
    out_specs = (P(GC, GR), P(GR, GC), P(GR, GC))
    return jax.shard_map(shards, mesh=fine, in_specs=in_specs, out_specs=out_specs, check_vma=False)
```

```python
import jax
import jax.numpy as jnp
from jax import lax
from jax.sharding import Mesh
from jax.sharding import PartitionSpec as P

STEP = 10


BETA_ONE = 0.9
BETA_TWO = 0.999
EPSILON = 1e-08

F32, BF16 = jnp.float32, jnp.bfloat16
LANES = 128
SIZES = {"y": 4, "zh": 2, "core": 2, "zf": 4, "zn": 2, "x": 4}
GR = ("y", "zh", "core")
GC = ("zf", "zn", "x")


def adam_step(rotated, first_moment, second_moment):
    new_first = BETA_ONE * first_moment + (1.0 - BETA_ONE) * rotated
    new_second = BETA_TWO * second_moment + (1.0 - BETA_TWO) * rotated * rotated
    corr_one = 1.0 - BETA_ONE**STEP
    corr_two = 1.0 - BETA_TWO**STEP
    direction = (new_first / corr_one / (jnp.sqrt(new_second / corr_two) + EPSILON)).astype(BF16)
    return (direction, new_first, new_second)


def spread(block, axes, n):
    return lax.all_to_all(jnp.broadcast_to(block[None], (n,) + block.shape), axes, 0, 0, tiled=True)


def swap(value, axis):
    return lax.ppermute(value, axis, [(0, 1), (1, 0)])


def shards(grad, basis, first_moment, second_moment):
    zh = lax.axis_index("zh")
    rows, cols = grad.shape
    block = grad.reshape(rows, cols // LANES, LANES)
    block = spread(block, "zf", 4)
    moments = jnp.stack([first_moment, second_moment])
    moments, block = lax.optimization_barrier((moments, block))
    slots = jnp.stack([jnp.where(zh == 0, 0.0, moments), jnp.where(zh == 0, moments, 0.0)])
    first_other, second_other = lax.psum_scatter(slots, "zh", scatter_dimension=0)
    block = spread(block, ("zn", "x"), 8)
    block = block.reshape(2, 2, 2, 4, rows, cols // LANES, LANES)
    picked = block.transpose(3, 1, 0, 2, 4, 5, 6).reshape(32 * rows, cols)

    partial = jnp.dot(picked, basis, preferred_element_type=F32).astype(BF16)
    parts = lax.all_to_all(partial.reshape(8, 80, -1), ("y", "core"), 0, 0, tiled=True)
    part = jnp.sum(parts.astype(F32), axis=0)
    rotated = part + swap(part.astype(BF16), "zh").astype(F32)
    low, high = rotated[:40], rotated[40:]
    first = zh == 0
    mine, other = jnp.where(first, low, high), jnp.where(first, high, low)
    share, new_first, new_second = adam_step(mine, first_moment, second_moment)
    share_other, _, _ = adam_step(other, first_other, second_other)
    pair = jnp.concatenate(
        [jnp.where(first, share, share_other), jnp.where(first, share_other, share)], axis=0
    )
    direction = lax.all_gather(pair, ("y", "core"), axis=0, tiled=True)

    total = lax.dot_general(
        direction, basis, (((1,), (1,)), ((), ())), preferred_element_type=F32
    ).astype(BF16)
    total = total.reshape(4, 2, 2, 2, rows, cols // LANES, LANES)
    total = total.transpose(2, 1, 3, 0, 4, 5, 6).reshape(8, 4, rows, cols // LANES, LANES)
    total = lax.all_to_all(total, ("zn", "x"), 0, 0, tiled=True)
    total = jnp.sum(total.astype(F32), axis=0).astype(BF16)
    total = lax.all_to_all(total, "zf", 0, 0, tiled=True)
    update = jnp.sum(total.astype(F32), axis=0).astype(BF16).reshape(rows, cols)
    return (update, new_first, new_second)


def solution(mesh):
    fine = Mesh(mesh.devices.reshape(tuple(SIZES.values())), tuple(SIZES))
    in_specs = (P(GC, GR), P(GR, GC), P(GR, GC), P(GR, GC))
    out_specs = (P(GC, GR), P(GR, GC), P(GR, GC))
    return jax.shard_map(shards, mesh=fine, in_specs=in_specs, out_specs=out_specs, check_vma=False)
```

```python
import jax
import jax.numpy as jnp
from jax import lax
from jax.sharding import Mesh
from jax.sharding import PartitionSpec as P

STEP = 10


BETA_ONE = 0.9
BETA_TWO = 0.999
EPSILON = 1e-08

F32, BF16 = jnp.float32, jnp.bfloat16
LANES = 128
SIZES = {"y": 4, "zh": 2, "core": 2, "zf": 4, "zn": 2, "x": 4}
GR = ("y", "zh", "core")
GC = ("zf", "zn", "x")


def adam_step(rotated, first_moment, second_moment):
    new_first = BETA_ONE * first_moment + (1.0 - BETA_ONE) * rotated
    new_second = BETA_TWO * second_moment + (1.0 - BETA_TWO) * rotated * rotated
    corr_one = 1.0 - BETA_ONE**STEP
    corr_two = 1.0 - BETA_TWO**STEP
    direction = (new_first / corr_one / (jnp.sqrt(new_second / corr_two) + EPSILON)).astype(BF16)
    return (direction, new_first, new_second)


def spread(block, axes, n):
    return lax.all_to_all(jnp.broadcast_to(block[None], (n,) + block.shape), axes, 0, 0, tiled=True)


def swap(value, axis):
    return lax.ppermute(value, axis, [(0, 1), (1, 0)])


def swap_cores(value, core):
    return lax.dynamic_index_in_dim(lax.all_gather(value, "core"), 1 - core, keepdims=False)


def shards(grad, basis, first_moment, second_moment):
    zh, core = lax.axis_index("zh"), lax.axis_index("core")
    rows, cols = grad.shape
    moments = swap(jnp.stack([first_moment, second_moment]).astype(BF16), "zh")

    block = grad.reshape(rows, cols // LANES, LANES)
    block = spread(block, "zf", 4)
    block, moments = lax.optimization_barrier((block, moments))
    first_other, second_other = moments[0].astype(F32), moments[1].astype(F32)
    block = spread(block, ("zn", "x"), 8)
    block = block.reshape(2, 2, 2, 4, rows, cols // LANES, LANES)
    picked = block.transpose(1, 3, 0, 2, 4, 5, 6).reshape(32 * rows, cols)

    partial = jnp.dot(picked, basis, preferred_element_type=F32).reshape(2, 320, -1)
    away = lax.dynamic_index_in_dim(partial, 1 - core, keepdims=False).astype(BF16)
    kept = lax.dynamic_index_in_dim(partial, core, keepdims=False)
    chip = (kept + swap_cores(away, core).astype(F32)).astype(BF16)
    parts = lax.all_to_all(chip.reshape(4, 80, -1), "y", 0, 0, tiled=True)
    part = jnp.sum(parts.astype(F32), axis=0)
    rotated = part + swap(part.astype(BF16), "zh").astype(F32)
    low, high = rotated[:40], rotated[40:]
    first = zh == 0
    mine, other = jnp.where(first, low, high), jnp.where(first, high, low)
    share, new_first, new_second = adam_step(mine, first_moment, second_moment)
    share_other, _, _ = adam_step(other, first_other, second_other)
    pair = jnp.concatenate(
        [jnp.where(first, share, share_other), jnp.where(first, share_other, share)], axis=0
    )
    direction = spread(pair, "y", 4).reshape(320, -1)
    direction = lax.all_gather(direction, "core", axis=0, tiled=True)

    total = lax.dot_general(
        direction, basis, (((1,), (1,)), ((), ())), preferred_element_type=F32
    ).astype(BF16)
    total = total.reshape(2, 4, 2, 2, rows, cols // LANES, LANES)
    total = total.transpose(2, 0, 3, 1, 4, 5, 6).reshape(8, 4, rows, cols // LANES, LANES)
    total = lax.all_to_all(total, ("zn", "x"), 0, 0, tiled=True)
    total = jnp.sum(total.astype(F32), axis=0).astype(BF16)
    total = lax.all_to_all(total, "zf", 0, 0, tiled=True)
    update = jnp.sum(total.astype(F32), axis=0).astype(BF16).reshape(rows, cols)
    return (update, new_first, new_second)


def solution(mesh):
    fine = Mesh(mesh.devices.reshape(tuple(SIZES.values())), tuple(SIZES))
    in_specs = (P(GC, GR), P(GR, GC), P(GR, GC), P(GR, GC))
    out_specs = (P(GC, GR), P(GR, GC), P(GR, GC))
    return jax.shard_map(shards, mesh=fine, in_specs=in_specs, out_specs=out_specs, check_vma=False)
```

```python
import jax
import jax.numpy as jnp
from jax import lax
from jax.sharding import Mesh
from jax.sharding import PartitionSpec as P

STEP = 10


BETA_ONE = 0.9
BETA_TWO = 0.999
EPSILON = 1e-08

F32, BF16 = jnp.float32, jnp.bfloat16
LANES = 128
SIZES = {"y": 4, "zh": 2, "core": 2, "zf": 4, "zn": 2, "x": 4}
GR = ("y", "zh", "core")
GC = ("zf", "zn", "x")


def adam_step(rotated, first_moment, second_moment):
    new_first = BETA_ONE * first_moment + (1.0 - BETA_ONE) * rotated
    new_second = BETA_TWO * second_moment + (1.0 - BETA_TWO) * rotated * rotated
    corr_one = 1.0 - BETA_ONE**STEP
    corr_two = 1.0 - BETA_TWO**STEP
    direction = (new_first / corr_one / (jnp.sqrt(new_second / corr_two) + EPSILON)).astype(BF16)
    return (direction, new_first, new_second)


def spread(block, axes, n):
    return lax.all_to_all(jnp.broadcast_to(block[None], (n,) + block.shape), axes, 0, 0, tiled=True)


def swap(value, axis):
    return lax.ppermute(value, axis, [(0, 1), (1, 0)])


def swap_cores(value, core):
    return lax.dynamic_index_in_dim(lax.all_gather(value, "core"), 1 - core, keepdims=False)


def shards(grad, basis, first_moment, second_moment):
    zh, core = lax.axis_index("zh"), lax.axis_index("core")
    rows, cols = grad.shape
    moments = jnp.stack([first_moment, second_moment]).astype(BF16)
    block = grad.reshape(rows, cols // LANES, LANES)
    block = spread(block, "zf", 4)
    block, moments = lax.optimization_barrier((block, moments))
    moments = swap(moments, "zh")
    block = spread(block, ("zn", "x"), 8)
    block, moments = lax.optimization_barrier((block, moments))
    first_other, second_other = moments[0].astype(F32), moments[1].astype(F32)
    block = block.reshape(2, 2, 2, 4, rows, cols // LANES, LANES)
    picked = block.transpose(1, 3, 0, 2, 4, 5, 6).reshape(32 * rows, cols)

    partial = jnp.dot(picked, basis, preferred_element_type=F32)
    away = lax.dynamic_slice_in_dim(partial, 320 * (1 - core), 320).astype(BF16)
    kept = lax.dynamic_slice_in_dim(partial, 320 * core, 320)
    chip = (kept + swap_cores(away, core).astype(F32)).astype(BF16)
    parts = lax.all_to_all(chip.reshape(4, 80, -1), "y", 0, 0, tiled=True)
    part = jnp.sum(parts.astype(F32), axis=0)
    rotated = part + swap(part.astype(BF16), "zh").astype(F32)
    low, high = rotated[:40], rotated[40:]
    first = zh == 0
    mine, other = jnp.where(first, low, high), jnp.where(first, high, low)
    share, new_first, new_second = adam_step(mine, first_moment, second_moment)
    share_other, _, _ = adam_step(other, first_other, second_other)
    pair = jnp.concatenate(
        [jnp.where(first, share, share_other), jnp.where(first, share_other, share)], axis=0
    )
    direction = spread(pair, "y", 4).reshape(320, -1)
    direction = lax.all_gather(direction, "core", axis=0, tiled=True)

    total = lax.dot_general(
        direction, basis, (((1,), (1,)), ((), ())), preferred_element_type=F32
    ).astype(BF16)
    total = total.reshape(2, 4, 2, 2, rows, cols // LANES, LANES)
    total = total.transpose(2, 0, 3, 1, 4, 5, 6).reshape(8, 4, rows, cols // LANES, LANES)
    total = lax.all_to_all(total, ("zn", "x"), 0, 0, tiled=True)
    total = jnp.sum(total.astype(F32), axis=0).astype(BF16)
    total = lax.all_to_all(total, "zf", 0, 0, tiled=True)
    update = jnp.sum(total.astype(F32), axis=0).astype(BF16).reshape(rows, cols)
    return (update, new_first, new_second)


def solution(mesh):
    fine = Mesh(mesh.devices.reshape(tuple(SIZES.values())), tuple(SIZES))
    in_specs = (P(GC, GR), P(GR, GC), P(GR, GC), P(GR, GC))
    out_specs = (P(GC, GR), P(GR, GC), P(GR, GC))
    return jax.shard_map(shards, mesh=fine, in_specs=in_specs, out_specs=out_specs, check_vma=False)
```

```python
import jax
import jax.numpy as jnp
from jax import lax
from jax.sharding import Mesh
from jax.sharding import PartitionSpec as P

STEP = 10


BETA_ONE = 0.9
BETA_TWO = 0.999
EPSILON = 1e-08

F32, BF16 = jnp.float32, jnp.bfloat16
LANES = 128
SIZES = {"y": 4, "zh": 2, "core": 2, "zf": 4, "zn": 2, "x": 4}
GR = ("y", "zh", "core")
GC = ("zf", "zn", "x")


def adam_step(rotated, first_moment, second_moment):
    new_first = BETA_ONE * first_moment + (1.0 - BETA_ONE) * rotated
    new_second = BETA_TWO * second_moment + (1.0 - BETA_TWO) * rotated * rotated
    corr_one = 1.0 - BETA_ONE**STEP
    corr_two = 1.0 - BETA_TWO**STEP
    direction = (new_first / corr_one / (jnp.sqrt(new_second / corr_two) + EPSILON)).astype(BF16)
    return (direction, new_first, new_second)


def spread(block, axes, n):
    return lax.all_to_all(jnp.broadcast_to(block[None], (n,) + block.shape), axes, 0, 0, tiled=True)


def swap(value, axis):
    return lax.ppermute(value, axis, [(0, 1), (1, 0)])


def swap_cores(value, core):
    return lax.dynamic_index_in_dim(lax.all_gather(value, "core"), 1 - core, keepdims=False)


def shards(grad, basis, first_moment, second_moment):
    zh, core = lax.axis_index("zh"), lax.axis_index("core")
    rows, cols = grad.shape
    moments = jnp.stack([first_moment, second_moment]).astype(BF16)
    block = grad.reshape(rows, cols // LANES, LANES)
    block = spread(block, "zf", 4)
    block = spread(block, ("zn", "x"), 8)
    block = block.reshape(2, 2, 2, 4, rows, cols // LANES, LANES)
    picked = block.transpose(1, 3, 0, 2, 4, 5, 6).reshape(32 * rows, cols)

    partial = jnp.dot(picked, basis, preferred_element_type=F32)
    away = lax.dynamic_slice_in_dim(partial, 320 * (1 - core), 320).astype(BF16)
    kept = lax.dynamic_slice_in_dim(partial, 320 * core, 320)
    chip = (kept + swap_cores(away, core).astype(F32)).astype(BF16)
    chip, moments = lax.optimization_barrier((chip, moments))
    first_other, second_other = swap(moments, "zh").astype(F32)
    parts = lax.all_to_all(chip.reshape(4, 80, -1), "y", 0, 0, tiled=True)
    part = jnp.sum(parts.astype(F32), axis=0)
    rotated = part + swap(part.astype(BF16), "zh").astype(F32)
    low, high = rotated[:40], rotated[40:]
    first = zh == 0
    mine, other = jnp.where(first, low, high), jnp.where(first, high, low)
    share, new_first, new_second = adam_step(mine, first_moment, second_moment)
    share_other, _, _ = adam_step(other, first_other, second_other)
    pair = jnp.concatenate(
        [jnp.where(first, share, share_other), jnp.where(first, share_other, share)], axis=0
    )
    direction = spread(pair, "y", 4).reshape(320, -1)
    direction = lax.all_gather(direction, "core", axis=0, tiled=True)

    total = lax.dot_general(
        direction, basis, (((1,), (1,)), ((), ())), preferred_element_type=F32
    ).astype(BF16)
    total = total.reshape(2, 4, 2, 2, rows, cols // LANES, LANES)
    total = total.transpose(2, 0, 3, 1, 4, 5, 6).reshape(8, 4, rows, cols // LANES, LANES)
    total = lax.all_to_all(total, ("zn", "x"), 0, 0, tiled=True)
    total = jnp.sum(total.astype(F32), axis=0).astype(BF16)
    total = lax.all_to_all(total, "zf", 0, 0, tiled=True)
    update = jnp.sum(total.astype(F32), axis=0).astype(BF16).reshape(rows, cols)
    return (update, new_first, new_second)


def solution(mesh):
    fine = Mesh(mesh.devices.reshape(tuple(SIZES.values())), tuple(SIZES))
    in_specs = (P(GC, GR), P(GR, GC), P(GR, GC), P(GR, GC))
    out_specs = (P(GC, GR), P(GR, GC), P(GR, GC))
    return jax.shard_map(shards, mesh=fine, in_specs=in_specs, out_specs=out_specs, check_vma=False)
```

```python
import jax
import jax.numpy as jnp
from jax import lax
from jax.sharding import Mesh
from jax.sharding import PartitionSpec as P

STEP = 10


BETA_ONE = 0.9
BETA_TWO = 0.999
EPSILON = 1e-08

F32, BF16 = jnp.float32, jnp.bfloat16
LANES = 128
SIZES = {"y": 4, "zh": 2, "core": 2, "zf": 4, "zn": 2, "x": 4}
GR = ("y", "zh", "core")
GC = ("zf", "zn", "x")


def adam_step(rotated, first_moment, second_moment):
    new_first = BETA_ONE * first_moment + (1.0 - BETA_ONE) * rotated
    new_second = BETA_TWO * second_moment + (1.0 - BETA_TWO) * rotated * rotated
    corr_one = 1.0 - BETA_ONE**STEP
    corr_two = 1.0 - BETA_TWO**STEP
    direction = (new_first / corr_one / (jnp.sqrt(new_second / corr_two) + EPSILON)).astype(BF16)
    return (direction, new_first, new_second)


def spread(block, axes, n):
    return lax.all_to_all(jnp.broadcast_to(block[None], (n,) + block.shape), axes, 0, 0, tiled=True)


def swap(value, axis):
    return lax.ppermute(value, axis, [(0, 1), (1, 0)])


def swap_cores(value, core):
    return lax.dynamic_index_in_dim(lax.all_gather(value, "core"), 1 - core, keepdims=False)


def shards(grad, basis, first_moment, second_moment):
    zh, core = lax.axis_index("zh"), lax.axis_index("core")
    rows, cols = grad.shape
    moments = swap(jnp.stack([first_moment, second_moment]).astype(BF16), "core")
    moments = lax.ppermute(moments, ("zh", "core"), [(i, 3 - i) for i in range(4)])
    block = grad.reshape(rows, cols // LANES, LANES)
    block = spread(block, "zf", 4)
    block = spread(block, ("zn", "x"), 8)
    block = block.reshape(2, 2, 2, 4, rows, cols // LANES, LANES)
    picked = block.transpose(1, 3, 0, 2, 4, 5, 6).reshape(32 * rows, cols)

    partial = jnp.dot(picked, basis, preferred_element_type=F32)
    away = lax.dynamic_slice_in_dim(partial, 320 * (1 - core), 320).astype(BF16)
    kept = lax.dynamic_slice_in_dim(partial, 320 * core, 320)
    chip = (kept + swap_cores(away, core).astype(F32)).astype(BF16)
    chip, moments = lax.optimization_barrier((chip, moments))
    first_other, second_other = moments.astype(F32)
    parts = lax.all_to_all(chip.reshape(4, 80, -1), "y", 0, 0, tiled=True)
    part = jnp.sum(parts.astype(F32), axis=0)
    rotated = part + swap(part.astype(BF16), "zh").astype(F32)
    low, high = rotated[:40], rotated[40:]
    first = zh == 0
    mine, other = jnp.where(first, low, high), jnp.where(first, high, low)
    share, new_first, new_second = adam_step(mine, first_moment, second_moment)
    share_other, _, _ = adam_step(other, first_other, second_other)
    pair = jnp.concatenate(
        [jnp.where(first, share, share_other), jnp.where(first, share_other, share)], axis=0
    )
    direction = spread(pair, "y", 4).reshape(320, -1)
    direction = lax.all_gather(direction, "core", axis=0, tiled=True)

    total = lax.dot_general(
        direction, basis, (((1,), (1,)), ((), ())), preferred_element_type=F32
    ).astype(BF16)
    total = total.reshape(2, 4, 2, 2, rows, cols // LANES, LANES)
    total = total.transpose(2, 0, 3, 1, 4, 5, 6).reshape(8, 4, rows, cols // LANES, LANES)
    total = lax.all_to_all(total, ("zn", "x"), 0, 0, tiled=True)
    total = jnp.sum(total.astype(F32), axis=0).astype(BF16)
    total = lax.all_to_all(total, "zf", 0, 0, tiled=True)
    update = jnp.sum(total.astype(F32), axis=0).astype(BF16).reshape(rows, cols)
    return (update, new_first, new_second)


def solution(mesh):
    fine = Mesh(mesh.devices.reshape(tuple(SIZES.values())), tuple(SIZES))
    in_specs = (P(GC, GR), P(GR, GC), P(GR, GC), P(GR, GC))
    out_specs = (P(GC, GR), P(GR, GC), P(GR, GC))
    return jax.shard_map(shards, mesh=fine, in_specs=in_specs, out_specs=out_specs, check_vma=False)
```

```python
import jax
import jax.numpy as jnp
from jax import lax
from jax.sharding import Mesh
from jax.sharding import PartitionSpec as P

STEP = 10


BETA_ONE = 0.9
BETA_TWO = 0.999
EPSILON = 1e-08

F32, BF16 = jnp.float32, jnp.bfloat16
LANES = 128
SIZES = {"y": 4, "zh": 2, "core": 2, "zf": 4, "zn": 2, "x1": 2, "x0": 2}
GR = ("y", "zh", "core")
GC = ("zf", "zn", "x1", "x0")


def adam_step(rotated, first_moment, second_moment):
    new_first = BETA_ONE * first_moment + (1.0 - BETA_ONE) * rotated
    new_second = BETA_TWO * second_moment + (1.0 - BETA_TWO) * rotated * rotated
    corr_one = 1.0 - BETA_ONE**STEP
    corr_two = 1.0 - BETA_TWO**STEP
    direction = (new_first / corr_one / (jnp.sqrt(new_second / corr_two) + EPSILON)).astype(BF16)
    return (direction, new_first, new_second)


def spread(block, axes, n):
    return lax.all_to_all(jnp.broadcast_to(block[None], (n,) + block.shape), axes, 0, 0, tiled=True)


def swap(value, axis):
    return lax.ppermute(value, axis, [(0, 1), (1, 0)])


def swap_cores(value, core):
    return lax.dynamic_index_in_dim(lax.all_gather(value, "core"), 1 - core, keepdims=False)


def shards(grad, basis, first_moment, second_moment):
    zh, core, x0 = lax.axis_index("zh"), lax.axis_index("core"), lax.axis_index("x0")
    rows, cols = grad.shape
    moments = jnp.stack([first_moment, second_moment]).astype(BF16)
    block = grad.reshape(rows, cols // LANES, LANES)
    block = spread(block, "zf", 4)
    block = spread(block, ("zn", "x1", "x0"), 8)
    block = block.reshape(2, 2, 2, 4, rows, cols // LANES, LANES)
    picked = block.transpose(1, 3, 0, 2, 4, 5, 6).reshape(32 * rows, cols)

    partial = jnp.dot(picked, basis, preferred_element_type=F32)
    away = lax.dynamic_slice_in_dim(partial, 320 * (1 - core), 320).astype(BF16)
    kept = lax.dynamic_slice_in_dim(partial, 320 * core, 320)
    chip = (kept + swap_cores(away, core).astype(F32)).astype(BF16)
    chip, moments, basis_sent = lax.optimization_barrier((chip, moments, basis))
    basis_next = swap(basis_sent, "x0")
    first_other, second_other = swap(moments, "zh").astype(F32)
    parts = lax.all_to_all(chip.reshape(4, 80, -1), "y", 0, 0, tiled=True)
    part = jnp.sum(parts.astype(F32), axis=0)
    rotated = part + swap(part.astype(BF16), "zh").astype(F32)
    low, high = rotated[:40], rotated[40:]
    first = zh == 0
    mine, other = jnp.where(first, low, high), jnp.where(first, high, low)
    share, new_first, new_second = adam_step(mine, first_moment, second_moment)
    share_other, _, _ = adam_step(other, first_other, second_other)
    pair = jnp.concatenate(
        [jnp.where(first, share, share_other), jnp.where(first, share_other, share)], axis=0
    )
    pair = pair.reshape(2, 2, rows, -1).transpose(1, 0, 2, 3).reshape(2, 2 * rows, -1)
    pair = jnp.broadcast_to(pair[None], (4,) + pair.shape).reshape(8, 2 * rows, -1)
    pair = lax.all_to_all(pair, ("y", "x0"), 0, 0, tiled=True).reshape(4, 2, 2 * rows, -1)
    direction = lax.all_gather(pair.transpose(1, 0, 2, 3), "core").reshape(2, 2, 8 * rows, -1)
    own = lax.dynamic_index_in_dim(direction, x0, 1, keepdims=False).reshape(16 * rows, -1)
    away = lax.dynamic_index_in_dim(direction, 1 - x0, 1, keepdims=False).reshape(16 * rows, -1)

    total = sum(
        lax.dot_general(d, b, (((1,), (1,)), ((), ())), preferred_element_type=F32)
        for d, b in ((own, basis), (away, basis_next))
    ).astype(BF16)
    total = total.reshape(2, 4, 2, rows, cols // LANES, LANES)
    total = total.transpose(2, 0, 1, 3, 4, 5).reshape(4, 4, rows, cols // LANES, LANES)
    total = lax.all_to_all(total, ("zn", "x1"), 0, 0, tiled=True)
    total = jnp.sum(total.astype(F32), axis=0).astype(BF16)
    total = lax.all_to_all(total, "zf", 0, 0, tiled=True)
    update = jnp.sum(total.astype(F32), axis=0).astype(BF16).reshape(rows, cols)
    return (update, new_first, new_second)


def solution(mesh):
    fine = Mesh(mesh.devices.reshape(tuple(SIZES.values())), tuple(SIZES))
    in_specs = (P(GC, GR), P(GR, GC), P(GR, GC), P(GR, GC))
    out_specs = (P(GC, GR), P(GR, GC), P(GR, GC))
    return jax.shard_map(shards, mesh=fine, in_specs=in_specs, out_specs=out_specs, check_vma=False)
```

```python
import jax
import jax.numpy as jnp
from jax import lax
from jax.sharding import Mesh
from jax.sharding import PartitionSpec as P

STEP = 10


BETA_ONE = 0.9
BETA_TWO = 0.999
EPSILON = 1e-08

F32, BF16 = jnp.float32, jnp.bfloat16
LANES = 128
SIZES = {"y": 4, "zh": 2, "core": 2, "zf": 4, "zn": 2, "x": 4}
GR = ("y", "zh", "core")
GC = ("zf", "zn", "x")


def adam_step(rotated, first_moment, second_moment):
    new_first = BETA_ONE * first_moment + (1.0 - BETA_ONE) * rotated
    new_second = BETA_TWO * second_moment + (1.0 - BETA_TWO) * rotated * rotated
    corr_one = 1.0 - BETA_ONE**STEP
    corr_two = 1.0 - BETA_TWO**STEP
    direction = (new_first / corr_one / (jnp.sqrt(new_second / corr_two) + EPSILON)).astype(BF16)
    return (direction, new_first, new_second)


def spread(block, axes, n):
    return lax.all_to_all(jnp.broadcast_to(block[None], (n,) + block.shape), axes, 0, 0, tiled=True)


def swap(value, axis):
    return lax.ppermute(value, axis, [(0, 1), (1, 0)])


def swap_gathered(value, axis):
    return lax.dynamic_index_in_dim(
        lax.all_gather(value, axis), 1 - lax.axis_index(axis), keepdims=False
    )


def shards(grad, basis, first_moment, second_moment):
    zh, core = lax.axis_index("zh"), lax.axis_index("core")
    rows, cols = grad.shape
    moments = swap(jnp.stack([first_moment, second_moment]).astype(BF16), "zh")
    block = grad.reshape(rows, cols // LANES, LANES)
    block = spread(block, "zf", 4)
    block = spread(block, ("zn", "x"), 8)
    block = block.reshape(2, 2, 2, 4, rows, cols // LANES, LANES)
    picked = block.transpose(1, 3, 0, 2, 4, 5, 6).reshape(32 * rows, cols)

    partial = jnp.dot(picked, basis, preferred_element_type=F32)
    away = lax.dynamic_slice_in_dim(partial, 320 * (1 - core), 320).astype(BF16)
    kept = lax.dynamic_slice_in_dim(partial, 320 * core, 320)
    chip = (kept + swap_gathered(away, "core").astype(F32)).astype(BF16)
    chip, moments = lax.optimization_barrier((chip, moments))
    first_other, second_other = moments.astype(F32)
    parts = lax.all_to_all(chip.reshape(4, 80, -1), "y", 0, 0, tiled=True)
    part = jnp.sum(parts.astype(F32), axis=0)
    rotated = part + swap_gathered(part.astype(BF16), "zh").astype(F32)
    low, high = rotated[:40], rotated[40:]
    first = zh == 0
    mine, other = jnp.where(first, low, high), jnp.where(first, high, low)
    share, new_first, new_second = adam_step(mine, first_moment, second_moment)
    share_other, _, _ = adam_step(other, first_other, second_other)
    pair = jnp.concatenate(
        [jnp.where(first, share, share_other), jnp.where(first, share_other, share)], axis=0
    )
    direction = spread(pair, "y", 4).reshape(320, -1)
    direction = lax.all_gather(direction, "core", axis=0, tiled=True)

    total = lax.dot_general(
        direction, basis, (((1,), (1,)), ((), ())), preferred_element_type=F32
    ).astype(BF16)
    total = total.reshape(2, 4, 2, 2, rows, cols // LANES, LANES)
    total = total.transpose(2, 0, 3, 1, 4, 5, 6).reshape(8, 4, rows, cols // LANES, LANES)
    total = lax.all_to_all(total, ("zn", "x"), 0, 0, tiled=True)
    total = jnp.sum(total.astype(F32), axis=0).astype(BF16)
    total = lax.all_to_all(total, "zf", 0, 0, tiled=True)
    update = jnp.sum(total.astype(F32), axis=0).astype(BF16).reshape(rows, cols)
    return (update, new_first, new_second)


def solution(mesh):
    fine = Mesh(mesh.devices.reshape(tuple(SIZES.values())), tuple(SIZES))
    in_specs = (P(GC, GR), P(GR, GC), P(GR, GC), P(GR, GC))
    out_specs = (P(GC, GR), P(GR, GC), P(GR, GC))
    return jax.shard_map(shards, mesh=fine, in_specs=in_specs, out_specs=out_specs, check_vma=False)
```

```python
import jax
import jax.numpy as jnp
from jax import lax
from jax.sharding import Mesh
from jax.sharding import PartitionSpec as P

STEP = 10


BETA_ONE = 0.9
BETA_TWO = 0.999
EPSILON = 1e-08

F32, BF16 = jnp.float32, jnp.bfloat16
LANES = 128
SIZES = {"y": 4, "zh": 2, "core": 2, "zf": 4, "zn": 2, "x": 4}
GR = ("y", "zh", "core")
GC = ("zf", "zn", "x")


def adam_step(rotated, first_moment, second_moment):
    new_first = BETA_ONE * first_moment + (1.0 - BETA_ONE) * rotated
    new_second = BETA_TWO * second_moment + (1.0 - BETA_TWO) * rotated * rotated
    corr_one = 1.0 - BETA_ONE**STEP
    corr_two = 1.0 - BETA_TWO**STEP
    direction = (new_first / corr_one / (jnp.sqrt(new_second / corr_two) + EPSILON)).astype(BF16)
    return (direction, new_first, new_second)


def spread(block, axes, n):
    return lax.all_to_all(jnp.broadcast_to(block[None], (n,) + block.shape), axes, 0, 0, tiled=True)


def swap(value, axis):
    return lax.ppermute(value, axis, [(0, 1), (1, 0)])


def swap_gathered(value, axis):
    return lax.dynamic_index_in_dim(
        lax.all_gather(value, axis), 1 - lax.axis_index(axis), keepdims=False
    )


def shards(grad, basis, first_moment, second_moment):
    zh, core = lax.axis_index("zh"), lax.axis_index("core")
    rows, cols = grad.shape
    first_other = swap(first_moment.astype(BF16), "zh")
    block = grad.reshape(rows, cols // LANES, LANES)
    block = spread(block, "zf", 4)
    block = spread(block, ("zn", "x"), 8)
    block = block.reshape(2, 2, 2, 4, rows, cols // LANES, LANES)
    picked = block.transpose(1, 3, 0, 2, 4, 5, 6).reshape(32 * rows, cols)

    partial = jnp.dot(picked, basis, preferred_element_type=F32)
    away = lax.dynamic_slice_in_dim(partial, 320 * (1 - core), 320).astype(BF16)
    kept = lax.dynamic_slice_in_dim(partial, 320 * core, 320)
    chip = (kept + swap_gathered(away, "core").astype(F32)).astype(BF16)
    chip, first_other, second_sent = lax.optimization_barrier((chip, first_other, second_moment))
    second_other = swap(second_sent.astype(BF16), "zh").astype(F32)
    first_other = first_other.astype(F32)
    parts = lax.all_to_all(chip.reshape(4, 80, -1), "y", 0, 0, tiled=True)
    part = jnp.sum(parts.astype(F32), axis=0)
    rotated = part + swap_gathered(part.astype(BF16), "zh").astype(F32)
    low, high = rotated[:40], rotated[40:]
    first = zh == 0
    mine, other = jnp.where(first, low, high), jnp.where(first, high, low)
    share, new_first, new_second = adam_step(mine, first_moment, second_moment)
    share_other, _, _ = adam_step(other, first_other, second_other)
    pair = jnp.concatenate(
        [jnp.where(first, share, share_other), jnp.where(first, share_other, share)], axis=0
    )
    direction = spread(pair, "y", 4).reshape(320, -1)
    direction = lax.all_gather(direction, "core", axis=0, tiled=True)

    total = lax.dot_general(
        direction, basis, (((1,), (1,)), ((), ())), preferred_element_type=F32
    ).astype(BF16)
    total = total.reshape(2, 4, 2, 2, rows, cols // LANES, LANES)
    total = total.transpose(2, 0, 3, 1, 4, 5, 6).reshape(8, 4, rows, cols // LANES, LANES)
    total = lax.all_to_all(total, ("zn", "x"), 0, 0, tiled=True)
    total = jnp.sum(total.astype(F32), axis=0).astype(BF16)
    total = lax.all_to_all(total, "zf", 0, 0, tiled=True)
    update = jnp.sum(total.astype(F32), axis=0).astype(BF16).reshape(rows, cols)
    return (update, new_first, new_second)


def solution(mesh):
    fine = Mesh(mesh.devices.reshape(tuple(SIZES.values())), tuple(SIZES))
    in_specs = (P(GC, GR), P(GR, GC), P(GR, GC), P(GR, GC))
    out_specs = (P(GC, GR), P(GR, GC), P(GR, GC))
    return jax.shard_map(shards, mesh=fine, in_specs=in_specs, out_specs=out_specs, check_vma=False)
```

```python
import jax
import jax.numpy as jnp
from jax import lax
from jax.sharding import Mesh
from jax.sharding import PartitionSpec as P

STEP = 10


BETA_ONE = 0.9
BETA_TWO = 0.999
EPSILON = 1e-08

F32, BF16 = jnp.float32, jnp.bfloat16
LANES = 128
SIZES = {"y": 4, "zh": 2, "core": 2, "zf": 4, "zn": 2, "x": 4}
GR = ("y", "zh", "core")
GC = ("zf", "zn", "x")


def adam_step(rotated, first_moment, second_moment):
    new_first = BETA_ONE * first_moment + (1.0 - BETA_ONE) * rotated
    new_second = BETA_TWO * second_moment + (1.0 - BETA_TWO) * rotated * rotated
    corr_one = 1.0 - BETA_ONE**STEP
    corr_two = 1.0 - BETA_TWO**STEP
    direction = (new_first / corr_one / (jnp.sqrt(new_second / corr_two) + EPSILON)).astype(BF16)
    return (direction, new_first, new_second)


def spread(block, axes, n):
    return lax.all_to_all(jnp.broadcast_to(block[None], (n,) + block.shape), axes, 0, 0, tiled=True)


def swap(value, axis):
    return lax.ppermute(value, axis, [(0, 1), (1, 0)])


def swap_gathered(value, axis):
    return lax.dynamic_index_in_dim(
        lax.all_gather(value, axis), 1 - lax.axis_index(axis), keepdims=False
    )


def shards(grad, basis, first_moment, second_moment):
    zh = lax.axis_index("zh")
    rows, cols = grad.shape
    block = grad.reshape(rows, cols // LANES, LANES)
    block = spread(block, "zf", 4)
    block = spread(block, ("zn", "x"), 8)
    block = block.reshape(2, 2, 2, 4, rows, cols // LANES, LANES)
    picked = block.transpose(3, 1, 0, 2, 4, 5, 6).reshape(32 * rows, cols)

    partial = jnp.dot(picked, basis, preferred_element_type=F32).astype(BF16)
    partial, *sent = lax.optimization_barrier((partial, first_moment, second_moment))
    moments = swap(jnp.stack(sent).astype(BF16), "zh")
    first_other, second_other = moments[0].astype(F32), moments[1].astype(F32)
    parts = lax.all_to_all(partial.reshape(8, 80, -1), ("y", "core"), 0, 0, tiled=True)
    part = jnp.sum(parts.astype(F32), axis=0)
    rotated = part + swap_gathered(part.astype(BF16), "zh").astype(F32)
    low, high = rotated[:40], rotated[40:]
    first = zh == 0
    mine, other = jnp.where(first, low, high), jnp.where(first, high, low)
    share, new_first, new_second = adam_step(mine, first_moment, second_moment)
    share_other, _, _ = adam_step(other, first_other, second_other)
    pair = jnp.concatenate(
        [jnp.where(first, share, share_other), jnp.where(first, share_other, share)], axis=0
    )
    direction = spread(pair, "y", 4).reshape(320, -1)
    direction = lax.all_gather(direction, "core", axis=0, tiled=True)

    total = lax.dot_general(
        direction, basis, (((1,), (1,)), ((), ())), preferred_element_type=F32
    ).astype(BF16)
    total = total.reshape(2, 4, 2, 2, rows, cols // LANES, LANES)
    total = total.transpose(2, 0, 3, 1, 4, 5, 6).reshape(8, 4, rows, cols // LANES, LANES)
    total = lax.all_to_all(total, ("zn", "x"), 0, 0, tiled=True)
    total = jnp.sum(total.astype(F32), axis=0).astype(BF16)
    total = lax.all_to_all(total, "zf", 0, 0, tiled=True)
    update = jnp.sum(total.astype(F32), axis=0).astype(BF16).reshape(rows, cols)
    return (update, new_first, new_second)


def solution(mesh):
    fine = Mesh(mesh.devices.reshape(tuple(SIZES.values())), tuple(SIZES))
    in_specs = (P(GC, GR), P(GR, GC), P(GR, GC), P(GR, GC))
    out_specs = (P(GC, GR), P(GR, GC), P(GR, GC))
    return jax.shard_map(shards, mesh=fine, in_specs=in_specs, out_specs=out_specs, check_vma=False)
```

```python
import jax
import jax.numpy as jnp
from jax import lax
from jax.sharding import Mesh
from jax.sharding import PartitionSpec as P

STEP = 10


BETA_ONE = 0.9
BETA_TWO = 0.999
EPSILON = 1e-08

F32, BF16 = jnp.float32, jnp.bfloat16
LANES = 128
SIZES = {"y": 4, "zh": 2, "core": 2, "zf": 4, "zn": 2, "x1": 2, "x0": 2}
GR = ("y", "zh", "core")
GC = ("zf", "zn", "x1", "x0")


def adam_step(rotated, first_moment, second_moment):
    new_first = BETA_ONE * first_moment + (1.0 - BETA_ONE) * rotated
    new_second = BETA_TWO * second_moment + (1.0 - BETA_TWO) * rotated * rotated
    corr_one = 1.0 - BETA_ONE**STEP
    corr_two = 1.0 - BETA_TWO**STEP
    direction = (new_first / corr_one / (jnp.sqrt(new_second / corr_two) + EPSILON)).astype(BF16)
    return (direction, new_first, new_second)


def spread(block, axes, n):
    return lax.all_to_all(jnp.broadcast_to(block[None], (n,) + block.shape), axes, 0, 0, tiled=True)


def swap(value, axis):
    return lax.ppermute(value, axis, [(0, 1), (1, 0)])


def swap_gathered(value, axis):
    return lax.dynamic_index_in_dim(
        lax.all_gather(value, axis), 1 - lax.axis_index(axis), keepdims=False
    )


def shards(grad, basis, first_moment, second_moment):
    zh, x0 = lax.axis_index("zh"), lax.axis_index("x0")
    rows, cols = grad.shape
    block = grad.reshape(rows, cols // LANES, LANES)
    block = spread(block, "zf", 4)
    block = spread(block, ("zn", "x1", "x0"), 8)
    block = block.reshape(2, 2, 2, 4, rows, cols // LANES, LANES)
    picked = block.transpose(3, 1, 0, 2, 4, 5, 6).reshape(32 * rows, cols)

    partial = jnp.dot(picked, basis, preferred_element_type=F32).astype(BF16)
    partial, *sent = lax.optimization_barrier((partial, first_moment, second_moment))
    basis_next = swap(basis, "x0")
    moments = swap(jnp.stack(sent).astype(BF16), "zh")
    first_other, second_other = moments[0].astype(F32), moments[1].astype(F32)
    parts = lax.all_to_all(partial.reshape(8, 80, -1), ("y", "core"), 0, 0, tiled=True)
    part = jnp.sum(parts.astype(F32), axis=0)
    rotated = part + swap_gathered(part.astype(BF16), "zh").astype(F32)
    low, high = rotated[:40], rotated[40:]
    first = zh == 0
    mine, other = jnp.where(first, low, high), jnp.where(first, high, low)
    share, new_first, new_second = adam_step(mine, first_moment, second_moment)
    share_other, _, _ = adam_step(other, first_other, second_other)
    pair = jnp.concatenate(
        [jnp.where(first, share, share_other), jnp.where(first, share_other, share)], axis=0
    )
    pair = pair.reshape(2, 2, rows, -1).transpose(1, 0, 2, 3).reshape(2, 2 * rows, -1)
    pair = jnp.broadcast_to(pair[None], (4,) + pair.shape).reshape(8, 2 * rows, -1)
    pair = lax.all_to_all(pair, ("y", "x0"), 0, 0, tiled=True).reshape(4, 2, 2 * rows, -1)
    direction = lax.all_gather(pair.transpose(1, 0, 2, 3), "core").reshape(2, 2, 8 * rows, -1)
    own = lax.dynamic_index_in_dim(direction, x0, 1, keepdims=False).reshape(16 * rows, -1)
    away = lax.dynamic_index_in_dim(direction, 1 - x0, 1, keepdims=False).reshape(16 * rows, -1)

    total = sum(
        lax.dot_general(d, b, (((1,), (1,)), ((), ())), preferred_element_type=F32)
        for d, b in ((own, basis), (away, basis_next))
    ).astype(BF16)
    total = total.reshape(2, 4, 2, rows, cols // LANES, LANES)
    total = total.transpose(2, 0, 1, 3, 4, 5).reshape(4, 4, rows, cols // LANES, LANES)
    total = lax.all_to_all(total, ("zn", "x1"), 0, 0, tiled=True)
    total = jnp.sum(total.astype(F32), axis=0).astype(BF16)
    total = lax.all_to_all(total, "zf", 0, 0, tiled=True)
    update = jnp.sum(total.astype(F32), axis=0).astype(BF16).reshape(rows, cols)
    return (update, new_first, new_second)


def solution(mesh):
    fine = Mesh(mesh.devices.reshape(tuple(SIZES.values())), tuple(SIZES))
    in_specs = (P(GC, GR), P(GR, GC), P(GR, GC), P(GR, GC))
    out_specs = (P(GC, GR), P(GR, GC), P(GR, GC))
    return jax.shard_map(shards, mesh=fine, in_specs=in_specs, out_specs=out_specs, check_vma=False)
```

```python
import jax
import jax.numpy as jnp
from jax import lax
from jax.sharding import Mesh
from jax.sharding import PartitionSpec as P

STEP = 10


BETA_ONE = 0.9
BETA_TWO = 0.999
EPSILON = 1e-08

F32, BF16 = jnp.float32, jnp.bfloat16
LANES = 128
SIZES = {"y": 4, "zh": 2, "core": 2, "zf": 4, "zn": 2, "x1": 2, "x0": 2}
GR = ("y", "zh", "core")
GC = ("zf", "zn", "x1", "x0")


def adam_step(rotated, first_moment, second_moment):
    new_first = BETA_ONE * first_moment + (1.0 - BETA_ONE) * rotated
    new_second = BETA_TWO * second_moment + (1.0 - BETA_TWO) * rotated * rotated
    corr_one = 1.0 - BETA_ONE**STEP
    corr_two = 1.0 - BETA_TWO**STEP
    direction = (new_first / corr_one / (jnp.sqrt(new_second / corr_two) + EPSILON)).astype(BF16)
    return (direction, new_first, new_second)


def spread(block, axes, n):
    return lax.all_to_all(jnp.broadcast_to(block[None], (n,) + block.shape), axes, 0, 0, tiled=True)


def swap(value, axis):
    return lax.ppermute(value, axis, [(0, 1), (1, 0)])


def swap_gathered(value, axis):
    return lax.dynamic_index_in_dim(
        lax.all_gather(value, axis), 1 - lax.axis_index(axis), keepdims=False
    )


def shards(grad, basis, first_moment, second_moment):
    zh, x0 = lax.axis_index("zh"), lax.axis_index("x0")
    rows, cols = grad.shape
    block = grad.reshape(rows, cols // LANES, LANES)
    block = spread(block, "zf", 4)
    block = spread(block, ("zn", "x1", "x0"), 8)
    block = block.reshape(2, 2, 2, 4, rows, cols // LANES, LANES)
    picked = block.transpose(3, 1, 0, 2, 4, 5, 6).reshape(32 * rows, cols)

    partial = jnp.dot(picked, basis, preferred_element_type=F32).astype(BF16)
    partial, *sent = lax.optimization_barrier((partial, first_moment, second_moment))
    basis_next = swap(basis, "x0")
    moments = swap(jnp.stack(sent).astype(BF16), "zh")
    first_other, second_other = moments[0].astype(F32), moments[1].astype(F32)
    parts = lax.all_to_all(partial.reshape(8, 80, -1), ("y", "core"), 0, 0, tiled=True)
    part = jnp.sum(parts.astype(F32), axis=0)
    rotated = part + swap_gathered(part.astype(BF16), "zh").astype(F32)
    low, high = rotated[:40], rotated[40:]
    first = zh == 0
    mine, other = jnp.where(first, low, high), jnp.where(first, high, low)
    share, new_first, new_second = adam_step(mine, first_moment, second_moment)
    share_other, _, _ = adam_step(other, first_other, second_other)
    pair = jnp.concatenate(
        [jnp.where(first, share, share_other), jnp.where(first, share_other, share)], axis=0
    )
    pair = pair.reshape(2, 2, rows, -1).transpose(1, 0, 2, 3).reshape(2, 2 * rows, -1)
    kept = lax.dynamic_index_in_dim(pair, x0, 0, keepdims=False)
    lent = lax.dynamic_index_in_dim(pair, 1 - x0, 0, keepdims=False)
    pair = spread(jnp.stack([kept, swap_gathered(lent, "x0")]), "y", 4)
    direction = lax.all_gather(pair.transpose(1, 0, 2, 3), "core")
    own, away = direction[:, 0].reshape(16 * rows, -1), direction[:, 1].reshape(16 * rows, -1)

    total = sum(
        lax.dot_general(d, b, (((1,), (1,)), ((), ())), preferred_element_type=F32)
        for d, b in ((own, basis), (away, basis_next))
    ).astype(BF16)
    total = total.reshape(2, 4, 2, rows, cols // LANES, LANES)
    total = total.transpose(2, 0, 1, 3, 4, 5).reshape(4, 4, rows, cols // LANES, LANES)
    total = lax.all_to_all(total, ("zn", "x1"), 0, 0, tiled=True)
    total = jnp.sum(total.astype(F32), axis=0).astype(BF16)
    total = lax.all_to_all(total, "zf", 0, 0, tiled=True)
    update = jnp.sum(total.astype(F32), axis=0).astype(BF16).reshape(rows, cols)
    return (update, new_first, new_second)


def solution(mesh):
    fine = Mesh(mesh.devices.reshape(tuple(SIZES.values())), tuple(SIZES))
    in_specs = (P(GC, GR), P(GR, GC), P(GR, GC), P(GR, GC))
    out_specs = (P(GC, GR), P(GR, GC), P(GR, GC))
    return jax.shard_map(shards, mesh=fine, in_specs=in_specs, out_specs=out_specs, check_vma=False)
```

```python
import jax
import jax.numpy as jnp
from jax import lax
from jax.sharding import Mesh
from jax.sharding import PartitionSpec as P

STEP = 10


BETA_ONE = 0.9
BETA_TWO = 0.999
EPSILON = 1e-08

F32, BF16 = jnp.float32, jnp.bfloat16
LANES = 128
SIZES = {"y": 4, "zh": 2, "core": 2, "zf": 4, "zn": 2, "x1": 2, "x0": 2}
GR = ("y", "zh", "core")
GC = ("zf", "zn", "x1", "x0")


def adam_step(rotated, first_moment, second_moment):
    new_first = BETA_ONE * first_moment + (1.0 - BETA_ONE) * rotated
    new_second = BETA_TWO * second_moment + (1.0 - BETA_TWO) * rotated * rotated
    corr_one = 1.0 - BETA_ONE**STEP
    corr_two = 1.0 - BETA_TWO**STEP
    direction = (new_first / corr_one / (jnp.sqrt(new_second / corr_two) + EPSILON)).astype(BF16)
    return (direction, new_first, new_second)


def spread(block, axes, n):
    return lax.all_to_all(jnp.broadcast_to(block[None], (n,) + block.shape), axes, 0, 0, tiled=True)


def swap(value, axis):
    return lax.ppermute(value, axis, [(0, 1), (1, 0)])


def swap_gathered(value, axis):
    return lax.dynamic_index_in_dim(
        lax.all_gather(value, axis), 1 - lax.axis_index(axis), keepdims=False
    )


def shards(grad, basis, first_moment, second_moment):
    zh, x0 = lax.axis_index("zh"), lax.axis_index("x0")
    rows, cols = grad.shape
    block = grad.reshape(rows, cols // LANES, LANES)
    block = spread(block, "zf", 4)
    block = spread(block, ("zn", "x1", "x0"), 8)
    block = block.reshape(2, 2, 2, 4, rows, cols // LANES, LANES)
    picked = block.transpose(3, 1, 0, 2, 4, 5, 6).reshape(32 * rows, cols)

    partial = jnp.dot(picked, basis, preferred_element_type=F32).astype(BF16)
    partial, *sent = lax.optimization_barrier((partial, first_moment, second_moment))
    basis_next = swap(basis, "x0")
    moments = swap(jnp.stack(sent).astype(BF16), "zh")
    first_other, second_other = moments[0].astype(F32), moments[1].astype(F32)
    parts = lax.all_to_all(partial.reshape(8, 80, -1), ("y", "core"), 0, 0, tiled=True)
    part = jnp.sum(parts.astype(F32), axis=0)
    rotated = part + swap_gathered(part.astype(BF16), "zh").astype(F32)
    low, high = rotated[:40], rotated[40:]
    first = zh == 0
    mine, other = jnp.where(first, low, high), jnp.where(first, high, low)
    share, new_first, new_second = adam_step(mine, first_moment, second_moment)
    share_other, _, _ = adam_step(other, first_other, second_other)
    pair = jnp.concatenate(
        [jnp.where(first, share, share_other), jnp.where(first, share_other, share)], axis=0
    )
    pair = pair.reshape(2, 2, rows, -1).transpose(1, 0, 2, 3).reshape(2, 2 * rows, -1)
    near, far = x0, 1 - x0
    pair, near, far = lax.optimization_barrier((pair, near, far))
    pair = jnp.broadcast_to(pair[None], (4,) + pair.shape).reshape(8, 2 * rows, -1)
    pair = lax.all_to_all(pair, ("y", "x0"), 0, 0, tiled=True).reshape(4, 2, 2 * rows, -1)
    direction = lax.all_gather(pair.transpose(1, 0, 2, 3), "core").reshape(2, 2, 8 * rows, -1)
    own, away = (
        lax.dynamic_index_in_dim(
            direction, i, 1, keepdims=False, allow_negative_indices=False
        ).reshape(16 * rows, -1)
        for i in (near, far)
    )

    total = sum(
        lax.dot_general(d, b, (((1,), (1,)), ((), ())), preferred_element_type=F32)
        for d, b in ((own, basis), (away, basis_next))
    ).astype(BF16)
    total = total.reshape(2, 4, 2, rows, cols // LANES, LANES)
    total = total.transpose(2, 0, 1, 3, 4, 5).reshape(4, 4, rows, cols // LANES, LANES)
    total = lax.all_to_all(total, ("zn", "x1"), 0, 0, tiled=True)
    total = jnp.sum(total.astype(F32), axis=0).astype(BF16)
    total = lax.all_to_all(total, "zf", 0, 0, tiled=True)
    update = jnp.sum(total.astype(F32), axis=0).astype(BF16).reshape(rows, cols)
    return (update, new_first, new_second)


def solution(mesh):
    fine = Mesh(mesh.devices.reshape(tuple(SIZES.values())), tuple(SIZES))
    in_specs = (P(GC, GR), P(GR, GC), P(GR, GC), P(GR, GC))
    out_specs = (P(GC, GR), P(GR, GC), P(GR, GC))
    return jax.shard_map(shards, mesh=fine, in_specs=in_specs, out_specs=out_specs, check_vma=False)
```

```python
import jax
import jax.numpy as jnp
from jax import lax
from jax.sharding import Mesh
from jax.sharding import PartitionSpec as P

STEP = 10


BETA_ONE = 0.9
BETA_TWO = 0.999
EPSILON = 1e-08

F32, BF16 = jnp.float32, jnp.bfloat16
LANES = 128
SIZES = {"y": 4, "zh": 2, "core": 2, "zf": 4, "zn": 2, "x1": 2, "x0": 2}
GR = ("y", "zh", "core")
GC = ("zf", "zn", "x1", "x0")


def adam_step(rotated, first_moment, second_moment):
    new_first = BETA_ONE * first_moment + (1.0 - BETA_ONE) * rotated
    new_second = BETA_TWO * second_moment + (1.0 - BETA_TWO) * rotated * rotated
    corr_one = 1.0 - BETA_ONE**STEP
    corr_two = 1.0 - BETA_TWO**STEP
    direction = (new_first / corr_one / (jnp.sqrt(new_second / corr_two) + EPSILON)).astype(BF16)
    return (direction, new_first, new_second)


def spread(block, axes, n):
    return lax.all_to_all(jnp.broadcast_to(block[None], (n,) + block.shape), axes, 0, 0, tiled=True)


def swap(value, axis):
    return lax.ppermute(value, axis, [(0, 1), (1, 0)])


def swap_gathered(value, axis):
    return lax.dynamic_index_in_dim(
        lax.all_gather(value, axis), 1 - lax.axis_index(axis), keepdims=False
    )


def shards(grad, basis, first_moment, second_moment):
    zh, x0 = lax.axis_index("zh"), lax.axis_index("x0")
    rows, cols = grad.shape
    block = grad.reshape(rows, cols // LANES, LANES)
    block = spread(block, "zf", 4)
    block = spread(block, ("zn", "x1", "x0"), 8)
    block = block.reshape(2, 2, 2, 4, rows, cols // LANES, LANES)
    picked = block.transpose(3, 1, 0, 2, 4, 5, 6).reshape(32 * rows, cols)

    partial = jnp.dot(picked, basis, preferred_element_type=F32).astype(BF16)
    partial, *sent = lax.optimization_barrier((partial, first_moment, second_moment))
    basis_next = swap(basis, "x0")
    moments = swap(jnp.stack(sent).astype(BF16), "zh")
    first_other, second_other = moments[0].astype(F32), moments[1].astype(F32)
    parts = lax.all_to_all(partial.reshape(8, 80, -1), ("y", "core"), 0, 0, tiled=True)
    part = jnp.sum(parts.astype(F32), axis=0)
    rotated = part + swap_gathered(part.astype(BF16), "zh").astype(F32)
    low, high = rotated[:40], rotated[40:]
    first = zh == 0
    mine, other = jnp.where(first, low, high), jnp.where(first, high, low)
    share, new_first, new_second = adam_step(mine, first_moment, second_moment)
    share_other, _, _ = adam_step(other, first_other, second_other)
    pair = jnp.concatenate(
        [jnp.where(first, share, share_other), jnp.where(first, share_other, share)], axis=0
    )
    pair = pair.reshape(2, 2, rows, -1).transpose(1, 0, 2, 3).reshape(2, 2 * rows, -1)
    near, far = x0, 1 - x0
    pair, near, far = lax.optimization_barrier((pair, near, far))
    pair = jnp.broadcast_to(pair[:, None], (2, 4, 2 * rows, pair.shape[-1]))
    pair = lax.all_to_all(pair.reshape(8, 2 * rows, -1), ("x0", "y"), 0, 0, tiled=True)
    direction = lax.all_gather(pair.reshape(2, 8 * rows, -1), "core")
    own, away = (
        lax.dynamic_index_in_dim(
            direction, i, 1, keepdims=False, allow_negative_indices=False
        ).reshape(16 * rows, -1)
        for i in (near, far)
    )

    total = sum(
        lax.dot_general(d, b, (((1,), (1,)), ((), ())), preferred_element_type=F32)
        for d, b in ((own, basis), (away, basis_next))
    ).astype(BF16)
    total = total.reshape(2, 4, 2, rows, cols // LANES, LANES)
    total = total.transpose(2, 0, 1, 3, 4, 5).reshape(4, 4, rows, cols // LANES, LANES)
    total = lax.all_to_all(total, ("zn", "x1"), 0, 0, tiled=True)
    total = jnp.sum(total.astype(F32), axis=0).astype(BF16)
    total = lax.all_to_all(total, "zf", 0, 0, tiled=True)
    update = jnp.sum(total.astype(F32), axis=0).astype(BF16).reshape(rows, cols)
    return (update, new_first, new_second)


def solution(mesh):
    fine = Mesh(mesh.devices.reshape(tuple(SIZES.values())), tuple(SIZES))
    in_specs = (P(GC, GR), P(GR, GC), P(GR, GC), P(GR, GC))
    out_specs = (P(GC, GR), P(GR, GC), P(GR, GC))
    return jax.shard_map(shards, mesh=fine, in_specs=in_specs, out_specs=out_specs, check_vma=False)
```

```python
import jax
import jax.numpy as jnp
from jax import lax
from jax.sharding import Mesh
from jax.sharding import PartitionSpec as P

STEP = 10


BETA_ONE = 0.9
BETA_TWO = 0.999
EPSILON = 1e-08

F32, BF16 = jnp.float32, jnp.bfloat16
LANES = 128
SIZES = {"y": 4, "zh": 2, "core": 2, "zf": 4, "zn": 2, "x1": 2, "x0": 2}
GR = ("y", "zh", "core")
GC = ("zf", "zn", "x1", "x0")


def adam_step(rotated, first_moment, second_moment):
    new_first = BETA_ONE * first_moment + (1.0 - BETA_ONE) * rotated
    new_second = BETA_TWO * second_moment + (1.0 - BETA_TWO) * rotated * rotated
    corr_one = 1.0 - BETA_ONE**STEP
    corr_two = 1.0 - BETA_TWO**STEP
    direction = (new_first / corr_one / (jnp.sqrt(new_second / corr_two) + EPSILON)).astype(BF16)
    return (direction, new_first, new_second)


def spread(block, axes, n):
    return lax.all_to_all(jnp.broadcast_to(block[None], (n,) + block.shape), axes, 0, 0, tiled=True)


def swap(value, axis):
    return lax.ppermute(value, axis, [(0, 1), (1, 0)])


def swap_gathered(value, axis):
    return lax.dynamic_index_in_dim(
        lax.all_gather(value, axis), 1 - lax.axis_index(axis), keepdims=False
    )


def shards(grad, basis, first_moment, second_moment):
    zh, x0 = lax.axis_index("zh"), lax.axis_index("x0")
    rows, cols = grad.shape
    block = grad.reshape(rows, cols // LANES, LANES)
    block = spread(block, "zf", 4)
    block = spread(block.reshape(4 * rows, cols), ("zn", "x1", "x0"), 8)
    partial = jnp.dot(block.reshape(32 * rows, cols), basis, preferred_element_type=F32)
    partial = partial.astype(BF16).reshape(2, 2, 2, 4, rows, -1)
    partial = partial.transpose(3, 1, 0, 2, 4, 5).reshape(32 * rows, -1)
    partial, *sent = lax.optimization_barrier((partial, first_moment, second_moment))
    basis_next = swap(basis, "x0")
    moments = swap(jnp.stack(sent).astype(BF16), "zh")
    first_other, second_other = moments[0].astype(F32), moments[1].astype(F32)
    parts = lax.all_to_all(partial.reshape(8, 80, -1), ("y", "core"), 0, 0, tiled=True)
    part = jnp.sum(parts.astype(F32), axis=0)
    rotated = part + swap_gathered(part.astype(BF16), "zh").astype(F32)
    low, high = rotated[:40], rotated[40:]
    first = zh == 0
    mine, other = jnp.where(first, low, high), jnp.where(first, high, low)
    share, new_first, new_second = adam_step(mine, first_moment, second_moment)
    share_other, _, _ = adam_step(other, first_other, second_other)
    pair = jnp.concatenate(
        [jnp.where(first, share, share_other), jnp.where(first, share_other, share)], axis=0
    )
    pair = pair.reshape(2, 2, rows, -1).transpose(1, 0, 2, 3).reshape(2, 2 * rows, -1)
    near, far = x0, 1 - x0
    pair, near, far = lax.optimization_barrier((pair, near, far))
    pair = jnp.broadcast_to(pair[:, None], (2, 4, 2 * rows, pair.shape[-1]))
    pair = lax.all_to_all(pair.reshape(8, 2 * rows, -1), ("x0", "y"), 0, 0, tiled=True)
    direction = lax.all_gather(pair.reshape(2, 8 * rows, -1), "core")
    own, away = (
        lax.dynamic_index_in_dim(
            direction, i, 1, keepdims=False, allow_negative_indices=False
        ).reshape(16 * rows, -1)
        for i in (near, far)
    )

    total = sum(
        lax.dot_general(d, b, (((1,), (1,)), ((), ())), preferred_element_type=F32)
        for d, b in ((own, basis), (away, basis_next))
    ).astype(BF16)
    total = total.reshape(2, 4, 2, rows, cols // LANES, LANES)
    total = total.transpose(2, 0, 1, 3, 4, 5).reshape(4, 4, rows, cols // LANES, LANES)
    total = lax.all_to_all(total, ("zn", "x1"), 0, 0, tiled=True)
    total = jnp.sum(total.astype(F32), axis=0).astype(BF16)
    total = lax.all_to_all(total, "zf", 0, 0, tiled=True)
    update = jnp.sum(total.astype(F32), axis=0).astype(BF16).reshape(rows, cols)
    return (update, new_first, new_second)


def solution(mesh):
    fine = Mesh(mesh.devices.reshape(tuple(SIZES.values())), tuple(SIZES))
    in_specs = (P(GC, GR), P(GR, GC), P(GR, GC), P(GR, GC))
    out_specs = (P(GC, GR), P(GR, GC), P(GR, GC))
    return jax.shard_map(shards, mesh=fine, in_specs=in_specs, out_specs=out_specs, check_vma=False)
```

```python
import jax
import jax.numpy as jnp
from jax import lax
from jax.sharding import Mesh
from jax.sharding import PartitionSpec as P

STEP = 10


BETA_ONE = 0.9
BETA_TWO = 0.999
EPSILON = 1e-08

F32, BF16 = jnp.float32, jnp.bfloat16
LANES = 128
SIZES = {"y": 4, "zh": 2, "core": 2, "zf": 4, "zn": 2, "x1": 2, "x0": 2}
GR = ("y", "zh", "core")
GC = ("zf", "zn", "x1", "x0")


def adam_step(rotated, first_moment, second_moment):
    new_first = BETA_ONE * first_moment + (1.0 - BETA_ONE) * rotated
    new_second = BETA_TWO * second_moment + (1.0 - BETA_TWO) * rotated * rotated
    corr_one = 1.0 - BETA_ONE**STEP
    corr_two = 1.0 - BETA_TWO**STEP
    direction = (new_first / corr_one / (jnp.sqrt(new_second / corr_two) + EPSILON)).astype(BF16)
    return (direction, new_first, new_second)


def spread(block, axes, n):
    return lax.all_to_all(jnp.broadcast_to(block[None], (n,) + block.shape), axes, 0, 0, tiled=True)


def swap(value, axis):
    return lax.ppermute(value, axis, [(0, 1), (1, 0)])


def swap_gathered(value, axis):
    return lax.dynamic_index_in_dim(
        lax.all_gather(value, axis), 1 - lax.axis_index(axis), keepdims=False
    )


def shards(grad, basis, first_moment, second_moment):
    zh, x0 = lax.axis_index("zh"), lax.axis_index("x0")
    rows, cols = grad.shape
    block = grad.reshape(rows, cols // LANES, LANES)
    block = spread(block, "zf", 4)
    block = spread(block.reshape(4 * rows, cols), ("zn", "x1", "x0"), 8)
    partial = jnp.dot(block.reshape(32 * rows, cols), basis, preferred_element_type=F32)
    partial = partial.reshape(2, 2, 2, 4, rows, -1)
    partial = partial.transpose(3, 1, 0, 2, 4, 5).reshape(32 * rows, -1).astype(BF16)
    partial, *sent = lax.optimization_barrier((partial, first_moment, second_moment))
    basis_next = swap(basis, "x0")
    moments = swap(jnp.stack(sent).astype(BF16), "zh")
    first_other, second_other = moments[0].astype(F32), moments[1].astype(F32)
    parts = lax.all_to_all(partial.reshape(8, 80, -1), ("y", "core"), 0, 0, tiled=True)
    part = jnp.sum(parts.astype(F32), axis=0)
    rotated = part + swap_gathered(part.astype(BF16), "zh").astype(F32)
    low, high = rotated[:40], rotated[40:]
    first = zh == 0
    mine, other = jnp.where(first, low, high), jnp.where(first, high, low)
    share, new_first, new_second = adam_step(mine, first_moment, second_moment)
    share_other, _, _ = adam_step(other, first_other, second_other)
    pair = jnp.concatenate(
        [jnp.where(first, share, share_other), jnp.where(first, share_other, share)], axis=0
    )
    pair = pair.reshape(2, 2, rows, -1).transpose(1, 0, 2, 3).reshape(2, 2 * rows, -1)
    near, far = x0, 1 - x0
    pair, near, far = lax.optimization_barrier((pair, near, far))
    pair = jnp.broadcast_to(pair[:, None], (2, 4, 2 * rows, pair.shape[-1]))
    pair = lax.all_to_all(pair.reshape(8, 2 * rows, -1), ("x0", "y"), 0, 0, tiled=True)
    direction = lax.all_gather(pair.reshape(2, 8 * rows, -1), "core")
    own, away = (
        lax.dynamic_index_in_dim(
            direction, i, 1, keepdims=False, allow_negative_indices=False
        ).reshape(16 * rows, -1)
        for i in (near, far)
    )

    total = sum(
        lax.dot_general(d, b, (((1,), (1,)), ((), ())), preferred_element_type=F32)
        for d, b in ((own, basis), (away, basis_next))
    ).astype(BF16)
    total = total.reshape(2, 4, 2, rows, cols // LANES, LANES)
    total = total.transpose(2, 0, 1, 3, 4, 5).reshape(4, 4, rows, cols // LANES, LANES)
    total = lax.all_to_all(total, ("zn", "x1"), 0, 0, tiled=True)
    total = jnp.sum(total.astype(F32), axis=0).astype(BF16)
    total = lax.all_to_all(total, "zf", 0, 0, tiled=True)
    update = jnp.sum(total.astype(F32), axis=0).astype(BF16).reshape(rows, cols)
    return (update, new_first, new_second)


def solution(mesh):
    fine = Mesh(mesh.devices.reshape(tuple(SIZES.values())), tuple(SIZES))
    in_specs = (P(GC, GR), P(GR, GC), P(GR, GC), P(GR, GC))
    out_specs = (P(GC, GR), P(GR, GC), P(GR, GC))
    return jax.shard_map(shards, mesh=fine, in_specs=in_specs, out_specs=out_specs, check_vma=False)
```
